768 devices in a mesh: dp: 24 (over z, core), tensor: 32 (over x, y).
Axes of the slice: x: 4, y: 8, z: 12, core: 2. Of those that a mesh axis runs over, the one named last changes fastest.
Arguments:
- gradient: bfloat16 [576, 512, 512], P('dp', 'tensor'), may hold values from -16000 to 16000
- momentum: float32 [576, 512, 512], P('dp', 'tensor'), may hold values from -4 to 4
- eig_left: bfloat16 [1536, 512, 512], P(('dp', 'tensor')), may hold values from -0.25 to 0.25
- eig_right: bfloat16 [1536, 512, 512], P(('dp', 'tensor')), may hold values from -0.25 to 0.25
- row_stats: float32 [1536, 512], P(('dp', 'tensor')), may hold values from 0.01 to 0.2
- col_stats: float32 [1536, 512], P(('dp', 'tensor')), may hold values from 0.01 to 0.2
- owners: int32 [576, 1], P('dp'), may hold values from 0 to 31; in each aligned block of 24 rows (0 to 23, 24 to 47, ...) at most 2 rows name the same one
Outputs:
- new_momentum: float32 [576, 512, 512], P('dp', 'tensor')
- update: bfloat16 [576, 512, 512], P('dp', 'tensor')
- new_rows: float32 [1536, 512], P(('dp', 'tensor'))
- new_cols: float32 [1536, 512], P(('dp', 'tensor'))
The draws below stay inside these ranges and needn't reach their ends.
Inputs may be any that keep to these rules, and one draw needn't show every extreme that they name: `owners`: among the 24 blocks of one data group no tensor index owns more than 2, and some index owns exactly 2.
All inputs are finite; a program needn't handle non-finite values.
Results may differ from the reference program's by a relative error of at most 0.0061.
Values may be sent and summed in bfloat16 or wider, within the bound.
A program may use at most 32 MiB of HBM per device.

```python
import math
import jax
import jax.numpy as jnp
import numpy as np
from jax import lax

BS = 512
OWN_MAX = 2
GB = 24
NB = 576
SLOTS = 1536
N_DP = 24
N_TENSOR = 32


def draw_gradient(key, part):
    key = jax.random.fold_in(key, 17)
    noise_key, block_key, row_key, col_key = jax.random.split(key, 4)
    block_scale = jnp.exp(jax.random.uniform(block_key, (NB, 1, 1), jnp.float32, 0.0, math.log(4.0)))
    rising = 1.0 + 2.0 * jnp.arange(NB, dtype=jnp.float32)[:, None, None] / max(NB - 1, 1)
    row_scale = jnp.exp(jax.random.uniform(row_key, (1, BS, 1), jnp.float32, 0.0, math.log(10.0)))
    col_scale = jnp.exp(jax.random.uniform(col_key, (1, 1, BS), jnp.float32, 0.0, math.log(10.0)))
    noise = jnp.clip(jax.random.normal(noise_key, (NB, BS, BS), jnp.float32), -6.0, 6.0)
    return (noise * block_scale * rising * row_scale * col_scale).astype(jnp.bfloat16)


def shard_levels(own_key, dims, pieces, smallest, largest):
    loudness, own = 1.0, jax.random.fold_in(own_key, 6)
    for position, blocks in pieces:
        draws = jnp.exp(jax.random.uniform(jax.random.fold_in(own, position), (blocks,), jnp.float32, smallest / len(pieces), largest / len(pieces)))
        loudness = loudness * jnp.repeat(draws, dims[position] // blocks).reshape([-1 if axis == position else 1 for axis in range(len(dims))])
    return loudness


def routed_block(stream_key, own, number, rows, number_of, top, limit, skew):
    sequence = jax.random.permutation(stream_key, number_of)
    crowded, ordinary = load_shares(number_of, rows * top, limit, skew, True), load_shares(number_of, rows * top, limit, skew, False)
    places = jnp.arange(number_of)

    def named(lengths, turn):
        used = int((lengths > 0).sum())
        fixed = max(1, used // 4)
        shifted = fixed + (places - fixed + turn * (used - fixed)) % max(1, number_of - fixed)
        return jnp.zeros((number_of,), jnp.int32).at[sequence[jnp.where(places < fixed, places, shifted)]].set(jnp.asarray(lengths, jnp.int32))

    lengths = jnp.where(number % 4 == 0, named(crowded, number // 4), named(ordinary, number - number // 4 - 1))
    mixed = jax.random.permutation(jax.random.fold_in(own, 3), number_of)
    giver, taker = mixed[0:number_of // 2 * 2:2], mixed[1:number_of // 2 * 2:2]
    room = jnp.minimum(lengths[giver] - 1, limit - lengths[taker]) // 2
    room = jnp.where((giver == sequence[0]) | (taker == sequence[0]) | (lengths[taker] == 0), 0, jnp.maximum(room, 0))
    shifted = jax.random.randint(jax.random.fold_in(own, 4), (number_of // 2,), 0, 1 << 20) % (room + 1)
    lengths = lengths.at[giver].add(-shifted).at[taker].add(shifted)
    labels = jnp.searchsorted(jnp.cumsum(lengths), jnp.arange(rows * top), side="right").astype(jnp.int32)
    table = labels.reshape(top, rows).T
    table = table[jax.random.permutation(jax.random.fold_in(own, 1), rows)]
    turn = jax.random.randint(jax.random.fold_in(own, 2), (rows, 1), 0, top)
    return jnp.take_along_axis(table, (jnp.arange(top)[None, :] + turn) % top, axis=1)


def load_shares(count, total, reach, slope, full):
    loads = [(1 << 20) // math.isqrt(standing ** slope) + 1 for standing in range(1, count + 1)]
    largest = reach if full else min(reach, max(-(-total // count), total * loads[0] // sum(loads)))
    least = 1 if total - largest >= count - 1 else 0
    given, spare = [largest] + [least] * (count - 1), total - largest - least * (count - 1)
    while spare > 0:
        movable = [i for i in range(1, count) if given[i] < largest] or [i for i in range(1, count) if given[i] < reach]
        pool, remaining = sum([loads[i] for i in movable]), spare
        for i in movable:
            more = min(reach - given[i], max(1, remaining * loads[i] // pool), spare)
            given[i] = given[i] + more
            spare = spare - more
    return np.array(given)


def gaussian(key, shape, spread, reach, shards=(), kind=jnp.bfloat16):
    entries = jax.random.normal(key, shape, jnp.float32) * spread
    if len(shards) > 0:
        entries = shard_levels(key, shape, shards, -0.22, 0.18) * entries
    return jnp.clip(entries, min=-reach, max=reach).astype(kind)


def setup_inputs(seed: int = 0) -> dict:
    seeds = jax.random.split(jax.random.key(seed), 8)
    gradient = draw_gradient(jax.random.fold_in(seeds[7], 71), 0)
    momentum = gaussian(seeds[1], (NB, BS, BS), 0.25, 4.0, ((0, 24), (1, 32)), jnp.float32)
    eig_left = gaussian(seeds[2], (SLOTS, BS, BS), BS ** -0.5, 0.25, ((0, 768),))
    eig_right = gaussian(seeds[3], (SLOTS, BS, BS), BS ** -0.5, 0.25, ((0, 768),))
    row_stats = jnp.clip(jnp.exp(math.log(0.2) - 2.9957323 * jax.random.uniform(seeds[4], (SLOTS, BS), jnp.float32) ** shard_levels(seeds[4], (SLOTS, BS), ((0, 768),), -0.2, 0.2)), 0.01, 0.2)
    col_stats = jnp.clip(jnp.exp(math.log(0.2) - 2.9957323 * jax.random.uniform(seeds[5], (SLOTS, BS), jnp.float32) ** shard_levels(seeds[5], (SLOTS, BS), ((0, 768),), -0.2, 0.2)), 0.01, 0.2)
    owners_keys = jax.random.split(jax.random.fold_in(seeds[6], 1), NB // GB)
    owners_turns = jax.random.permutation(jax.random.fold_in(seeds[6], 3), NB // GB)
    owners = jax.vmap(lambda own, number: routed_block(jax.random.fold_in(seeds[6], 2), own, number, GB, N_TENSOR, 1, OWN_MAX, 2))(owners_keys, owners_turns).reshape((NB, 1))
    return {"gradient": gradient, "momentum": momentum, "eig_left": eig_left, "eig_right": eig_right, "row_stats": row_stats, "col_stats": col_stats, "owners": owners}


momentum_decay = 0.9
second_decay = 0.95
epsilon = 1e-08
clip_share = 0.25

def block_slots(owners):
    groups = owners[:, 0].reshape(N_DP, GB).astype(jnp.int32)
    counter = jnp.arange(GB, dtype=jnp.int32)
    same_owner = groups[:, :, None] == groups[:, None, :]
    before = counter[None, :] < counter[:, None]
    earlier_count = lax.optimization_barrier(jnp.sum((same_owner & before[None]).astype(jnp.int32), axis=2))
    row_ids = jnp.arange(N_DP, dtype=jnp.int32)[:, None]
    return ((row_ids * N_TENSOR + groups) * OWN_MAX + earlier_count).reshape(NB).astype(jnp.int32)

def reference(gradient, momentum, eig_left, eig_right, row_stats, col_stats, owners):
    widened = gradient.astype(jnp.float32)
    squared_sum = jnp.sum(widened * widened)
    factor = jnp.minimum(1.0, clip_share * BS * math.sqrt(NB) / jnp.sqrt(squared_sum))
    clipped = widened * factor
    new_momentum = momentum_decay * momentum + (1.0 - momentum_decay) * clipped
    sent_grad = clipped.astype(jnp.bfloat16)
    sent_moment = new_momentum.astype(jnp.bfloat16)
    slot_place = block_slots(owners)

    def one_block(inputs):
        grad_block, moment_block, slot_here = inputs
        left_basis = eig_left[slot_here]
        right_basis = eig_right[slot_here]
        half_grad = jnp.dot(left_basis.T, grad_block, preferred_element_type=jnp.float32).astype(jnp.bfloat16)
        half_moment = jnp.dot(left_basis.T, moment_block, preferred_element_type=jnp.float32).astype(jnp.bfloat16)
        rot_grad = jnp.dot(half_grad, right_basis, preferred_element_type=jnp.float32)
        rot_moment = jnp.dot(half_moment, right_basis, preferred_element_type=jnp.float32)
        squares = rot_grad * rot_grad
        rows_next = second_decay * row_stats[slot_here] + (1.0 - second_decay) * lax.optimization_barrier(jnp.mean(squares, axis=1))
        cols_next = second_decay * col_stats[slot_here] + (1.0 - second_decay) * lax.optimization_barrier(jnp.mean(squares, axis=0))
        scale_hat = rows_next[:, None] * cols_next[None, :] / jnp.mean(rows_next)
        direction = (rot_moment / (jnp.sqrt(scale_hat) + epsilon)).astype(jnp.bfloat16)
        half_back = jnp.dot(left_basis, direction, preferred_element_type=jnp.float32).astype(jnp.bfloat16)
        finished = jnp.dot(half_back, right_basis.T, preferred_element_type=jnp.float32).astype(jnp.bfloat16)
        return (finished, rows_next, cols_next)
    update, rows_all, cols_all = lax.map(one_block, (sent_grad, sent_moment, slot_place))
    new_rows = row_stats.at[slot_place].set(rows_all)
    new_cols = col_stats.at[slot_place].set(cols_all)
    return (new_momentum, update, new_rows, new_cols)
```

```python
import functools
import math

import jax
import jax.numpy as jnp
from jax import lax
from jax.experimental import pallas as pl
from jax.experimental.pallas import tpu as pltpu
from jax.sharding import PartitionSpec as P

momentum_decay = 0.9
second_decay = 0.95
epsilon = 1e-08
clip_share = 0.25
columns = 8
chunk = 128
MESH = pl.DeviceIdType.MESH
f32 = jnp.float32
bf16 = jnp.bfloat16


def dot(a, b):
    return jnp.dot(a, b, preferred_element_type=f32)


def to_column(row):
    return jnp.broadcast_to(row, (128, row.shape[1])).T[:, 0:1]


def to_row(column):
    return jnp.broadcast_to(column, (column.shape[0], 128)).T[0:1, :]


def kernel(
    n_dp,
    n_tensor,
    clip_norm,
    owners,
    gradient,
    momentum,
    left,
    right,
    row_stats,
    col_stats,
    new_momentum,
    update,
    new_rows,
    new_cols,
    grad_v,
    mom_v,
    moment_v,
    update_v,
    left_v,
    right_v,
    left_t,
    right_t,
    inverse,
    out_g,
    out_m,
    out_u,
    in_g,
    in_m,
    in_u,
    sums_t,
    sums_d,
    chosen_v,
    chosen,
    local_sem,
    send_sem,
    recv_sem,
):
    blocks, strip, size = grad_v.shape
    me = lax.axis_index("tensor")
    group = lax.axis_index("dp")
    my_x = me // columns
    my_y = lax.rem(me, columns)
    barrier = pltpu.get_barrier_semaphore()

    @pl.loop(1, n_tensor)
    def _(i):
        pl.semaphore_signal(
            barrier, inc=1, device_id={"tensor": lax.rem(me + i, n_tensor)}, device_id_type=MESH
        )

    @pl.loop(1, n_dp)
    def _(i):
        pl.semaphore_signal(
            barrier, inc=1, device_id={"dp": lax.rem(group + i, n_dp)}, device_id_type=MESH
        )

    load_g = pltpu.make_async_copy(gradient, grad_v, local_sem.at[0])
    load_m = pltpu.make_async_copy(momentum, mom_v, local_sem.at[1])
    load_l = pltpu.make_async_copy(left, left_v, local_sem.at[2])
    load_r = pltpu.make_async_copy(right, right_v, local_sem.at[3])
    load_g.start()
    load_m.start()
    load_l.start()
    load_r.start()

    lane = lax.broadcasted_iota(jnp.int32, (8, 128), 1)
    level = lax.broadcasted_iota(jnp.int32, (8, 128), 0)
    first = jnp.full((8, 128), -1, jnp.int32)
    second = first
    for b in range(blocks):
        mine = lane == owners[b, 0]
        second = jnp.where(mine & (first >= 0), b, second)
        first = jnp.where(mine & (first < 0), b, first)
    chosen_v[...] = jnp.where(level == 0, first, second)
    load_c = pltpu.make_async_copy(chosen_v, chosen, local_sem.at[4])
    load_c.start()
    load_g.wait()

    def squares(b, total):
        wide = grad_v[b].astype(f32)
        wide = wide * wide
        for j in range(size // 128):
            for i in range(strip // 8):
                total = total + wide[8 * i : 8 * i + 8, 128 * j : 128 * j + 128]
        return total

    sums_t[me] = lax.fori_loop(0, blocks, squares, jnp.zeros((8, 128), f32))
    load_c.wait()

    def pack(source, target):
        @pl.loop(0, n_tensor)
        def _(p):
            for k in range(2):
                target[k, p] = source[jnp.maximum(chosen[k, p], 0)]

    def strip_of(p):
        return pl.ds(pl.multiple_of(p * strip, strip), strip)

    def scatter(source, target, k, number):
        @pl.loop(1, n_tensor)
        def _(i):
            dx = i // columns
            j = lax.rem(i, columns)
            odd = lax.rem(j, 2)
            dy = odd * ((j + 1) // 2) + (1 - odd) * lax.rem(columns - j // 2, columns)
            p = lax.rem(my_x + dx, n_tensor // columns) * columns + lax.rem(my_y + dy, columns)
            pltpu.make_async_remote_copy(
                src_ref=source.at[k, p],
                dst_ref=target.at[k, strip_of(me)],
                send_sem=send_sem.at[number],
                recv_sem=recv_sem.at[number],
                device_id={"tensor": p},
                device_id_type=MESH,
            ).start()

    def waiter(ref, number):
        return pltpu.make_async_remote_copy(
            src_ref=ref,
            dst_ref=ref,
            send_sem=send_sem.at[number],
            recv_sem=recv_sem.at[number],
            device_id={"tensor": lax.rem(me + 1, n_tensor)},
            device_id_type=MESH,
        )

    others = pl.ds(0, (n_tensor - 1) * strip)
    pack(grad_v, out_g)
    pl.semaphore_wait(barrier, n_tensor + n_dp - 2)

    @pl.loop(1, n_tensor)
    def _(i):
        pltpu.make_async_remote_copy(
            src_ref=sums_t.at[me],
            dst_ref=sums_t.at[me],
            send_sem=send_sem.at[0],
            recv_sem=recv_sem.at[0],
            device_id={"tensor": lax.rem(me + i, n_tensor)},
            device_id_type=MESH,
        ).start()

    scatter(out_g, in_g, 0, 2)
    in_g[0, strip_of(me)] = out_g[0, me]
    in_g[1, strip_of(me)] = out_g[1, me]
    waiter(sums_t.at[pl.ds(0, n_tensor - 1)], 0).wait_recv()
    sums_d[group] = jnp.sum(sums_t[...], axis=0)

    @pl.loop(1, n_dp)
    def _(i):
        pltpu.make_async_remote_copy(
            src_ref=sums_d.at[group],
            dst_ref=sums_d.at[group],
            send_sem=send_sem.at[1],
            recv_sem=recv_sem.at[1],
            device_id={"dp": lax.rem(group + i, n_dp)},
            device_id_type=MESH,
        ).start()

    scatter(out_g, in_g, 1, 3)
    load_l.wait()
    load_r.wait()
    for k in range(2):
        left_t[k] = left_v[k].T
        right_t[k] = right_v[k].T
    load_m.wait()
    waiter(sums_d.at[pl.ds(0, n_dp - 1)], 1).wait_recv()
    squared_sum = jnp.sum(jnp.sum(sums_d[...], axis=0), keepdims=True)
    limit = clip_norm * clip_norm
    factor = jnp.where(
        squared_sum > limit, clip_norm / jnp.sqrt(jnp.maximum(squared_sum, limit)), 1.0
    )

    @pl.loop(0, blocks)
    def _(b):
        clipped = grad_v[b].astype(f32) * factor
        moved = momentum_decay * mom_v[b] + (1.0 - momentum_decay) * clipped
        mom_v[b] = moved
        moment_v[b] = moved.astype(bf16)

    store_m = pltpu.make_async_copy(mom_v, new_momentum, local_sem.at[1])
    store_m.start()
    pack(moment_v, out_m)
    for k in range(2):
        scatter(out_m, in_m, k, 4 + k)
        in_m[k, strip_of(me)] = out_m[k, me]

    share = factor * factor * ((1.0 - second_decay) / size)
    for k in range(2):
        waiter(in_g.at[k, others], 2 + k).wait_recv()
        half = dot(left_t[k], in_g[k]).astype(bf16)
        rotated = dot(half, right_v[k])
        square = rotated * rotated
        rows_old = row_stats[k : k + 1, :]
        cols_old = col_stats[k : k + 1, :]
        rows_next = second_decay * to_column(rows_old) + share * jnp.sum(
            square, axis=1, keepdims=True
        )
        cols_next = second_decay * cols_old + share * jnp.sum(square, axis=0, keepdims=True)
        mean = jnp.sum(rows_next, axis=0, keepdims=True) * (1.0 / size)
        inverse[k] = 1.0 / (jnp.sqrt(rows_next / mean) * jnp.sqrt(cols_next) + epsilon)
        used = jnp.full((1, size), chosen[k, me], jnp.int32) >= 0
        new_rows[k : k + 1, :] = jnp.where(used, to_row(rows_next), rows_old)
        new_cols[k : k + 1, :] = jnp.where(used, cols_next, cols_old)

    for k in range(2):
        waiter(in_m.at[k, others], 4 + k).wait_recv()
        half = dot(left_t[k], in_m[k]).astype(bf16)
        direction = (dot(half, right_v[k]) * inverse[k]).astype(bf16)
        for j in range(n_tensor // columns):
            c = lax.rem(my_x + j, n_tensor // columns)
            band = pl.ds(pl.multiple_of(c * chunk, chunk), chunk)
            half_back = dot(left_v[k, band], direction).astype(bf16)
            out_u[k, band] = dot(half_back, right_t[k]).astype(bf16)

            @pl.loop(1 if j == 0 else 0, columns)
            def _(i):
                p = c * columns + lax.rem(my_y + i, columns)
                pltpu.make_async_remote_copy(
                    src_ref=out_u.at[k, strip_of(p)],
                    dst_ref=in_u.at[k, me],
                    send_sem=send_sem.at[6 + k],
                    recv_sem=recv_sem.at[6 + k],
                    device_id={"tensor": p},
                    device_id_type=MESH,
                ).start()

        in_u[k, me] = out_u[k, strip_of(me)]

    for k in range(2):
        waiter(in_u.at[k, pl.ds(0, n_tensor - 1)], 6 + k).wait_recv()

    @pl.loop(0, blocks)
    def _(b):
        o = owners[b, 0]
        rank = (chosen[0, o] != b).astype(jnp.int32)
        update_v[b] = in_u[rank, o]

    store_u = pltpu.make_async_copy(update_v, update, local_sem.at[0])
    store_u.start()
    waiter(sums_t.at[pl.ds(0, n_tensor - 1)], 0).wait_send()
    waiter(sums_d.at[pl.ds(0, n_dp - 1)], 1).wait_send()
    for k in range(2):
        waiter(in_g.at[k, others], 2 + k).wait_send()
        waiter(in_m.at[k, others], 4 + k).wait_send()
        waiter(in_u.at[k, pl.ds(0, n_tensor - 1)], 6 + k).wait_send()
    store_m.wait()
    store_u.wait()


def local(n_dp, n_tensor, gradient, momentum, eig_left, eig_right, row_stats, col_stats, owners):
    blocks, strip, size = gradient.shape
    slots = eig_left.shape[0]
    clip_norm = clip_share * size * math.sqrt(blocks * n_dp)
    anywhere = pl.BlockSpec(memory_space=pl.ANY)
    vmem = pl.BlockSpec(memory_space=pltpu.VMEM)
    square = (slots, size, size)
    pieces = (slots, n_tensor, strip, size)
    return pl.pallas_call(
        functools.partial(kernel, n_dp, n_tensor, clip_norm),
        out_shape=(
            jax.ShapeDtypeStruct(momentum.shape, f32),
            jax.ShapeDtypeStruct(gradient.shape, bf16),
            jax.ShapeDtypeStruct(row_stats.shape, f32),
            jax.ShapeDtypeStruct(col_stats.shape, f32),
        ),
        in_specs=[
            pl.BlockSpec(memory_space=pltpu.SMEM),
            anywhere,
            anywhere,
            anywhere,
            anywhere,
            vmem,
            vmem,
        ],
        out_specs=(anywhere, anywhere, vmem, vmem),
        scratch_shapes=[
            pltpu.VMEM(gradient.shape, bf16),
            pltpu.VMEM(gradient.shape, f32),
            pltpu.VMEM(gradient.shape, bf16),
            pltpu.VMEM(gradient.shape, bf16),
            pltpu.VMEM(square, bf16),
            pltpu.VMEM(square, bf16),
            pltpu.VMEM(square, bf16),
            pltpu.VMEM(square, bf16),
            pltpu.VMEM(square, f32),
            pltpu.VMEM(pieces, bf16),
            pltpu.VMEM(pieces, bf16),
            pltpu.VMEM(square, bf16),
            pltpu.VMEM(square, bf16),
            pltpu.VMEM(square, bf16),
            pltpu.VMEM(pieces, bf16),
            pltpu.VMEM((n_tensor, 8, 128), f32),
            pltpu.VMEM((n_dp, 8, 128), f32),
            pltpu.VMEM((8, 128), jnp.int32),
            pltpu.SMEM((8, 128), jnp.int32),
            pltpu.SemaphoreType.DMA((5,)),
            pltpu.SemaphoreType.DMA((8,)),
            pltpu.SemaphoreType.DMA((8,)),
        ],
        compiler_params=pltpu.CompilerParams(
            collective_id=0, has_side_effects=True, vmem_limit_bytes=48 << 20
        ),
        name="soap_step",
    )(owners, gradient, momentum, eig_left, eig_right, row_stats, col_stats)


def solution(mesh):
    placed = (
        P("dp", "tensor", None),
        P("dp", "tensor", None),
        P(("dp", "tensor"), None, None),
        P(("dp", "tensor"), None, None),
        P(("dp", "tensor"), None),
        P(("dp", "tensor"), None),
        P("dp", None),
    )
    return jax.shard_map(
        functools.partial(local, mesh.shape["dp"], mesh.shape["tensor"]),
        mesh=mesh,
        in_specs=placed,
        out_specs=(
            P("dp", "tensor", None),
            P("dp", "tensor", None),
            P(("dp", "tensor"), None),
            P(("dp", "tensor"), None),
        ),
        check_vma=False,
    )
```

```python
import functools
import math

import jax
import jax.numpy as jnp
from jax import lax
from jax.experimental import pallas as pl
from jax.experimental.pallas import tpu as pltpu
from jax.sharding import PartitionSpec as P

momentum_decay = 0.9
second_decay = 0.95
epsilon = 1e-08
clip_share = 0.25
columns = 8
lead = 11
chunk = 128
MESH = pl.DeviceIdType.MESH
f32 = jnp.float32
bf16 = jnp.bfloat16


def dot(a, b):
    return jnp.dot(a, b, preferred_element_type=f32)


def to_column(row):
    return jnp.broadcast_to(row, (128, row.shape[1])).T[:, 0:1]


def to_row(column):
    return jnp.broadcast_to(column, (column.shape[0], 128)).T[0:1, :]


def kernel(
    n_dp,
    n_tensor,
    clip_norm,
    owners,
    gradient,
    momentum,
    left,
    right,
    row_stats,
    col_stats,
    new_momentum,
    update,
    new_rows,
    new_cols,
    grad_v,
    mom_v,
    moment_v,
    update_v,
    left_v,
    right_v,
    left_t,
    right_t,
    inverse,
    out_g,
    out_m,
    out_u,
    in_g,
    in_m,
    in_u,
    sums_t,
    sums_d,
    total,
    chosen_v,
    chosen,
    local_sem,
    send_sem,
    recv_sem,
):
    blocks, strip, size = grad_v.shape
    me = lax.axis_index("tensor")
    group = lax.axis_index("dp")
    my_x = me // columns
    my_y = lax.rem(me, columns)
    barrier = pltpu.get_barrier_semaphore()

    @pl.loop(1, n_tensor)
    def _(i):
        pl.semaphore_signal(
            barrier, inc=1, device_id={"tensor": lax.rem(me + i, n_tensor)}, device_id_type=MESH
        )

    @pl.when(me == lead)
    def _():
        @pl.loop(1, n_dp)
        def _(i):
            pl.semaphore_signal(
                barrier, inc=1, device_id={"dp": lax.rem(group + i, n_dp)}, device_id_type=MESH
            )

    load_g = pltpu.make_async_copy(gradient, grad_v, local_sem.at[0])
    load_m = pltpu.make_async_copy(momentum, mom_v, local_sem.at[1])
    load_l = pltpu.make_async_copy(left, left_v, local_sem.at[2])
    load_r = pltpu.make_async_copy(right, right_v, local_sem.at[3])
    load_g.start()
    load_m.start()
    load_l.start()
    load_r.start()

    lane = lax.broadcasted_iota(jnp.int32, (8, 128), 1)
    level = lax.broadcasted_iota(jnp.int32, (8, 128), 0)
    first = jnp.full((8, 128), -1, jnp.int32)
    second = first
    for b in range(blocks):
        mine = lane == owners[0, b]
        second = jnp.where(mine & (first >= 0), b, second)
        first = jnp.where(mine & (first < 0), b, first)
    chosen_v[...] = jnp.where(level == 0, first, second)
    load_c = pltpu.make_async_copy(chosen_v, chosen, local_sem.at[4])
    load_c.start()
    load_g.wait()

    def squares(b, total):
        wide = grad_v[b].astype(f32)
        wide = wide * wide
        for j in range(size // 128):
            for i in range(strip // 8):
                total = total + wide[8 * i : 8 * i + 8, 128 * j : 128 * j + 128]
        return total

    mine = lax.fori_loop(0, blocks, squares, jnp.zeros((8, 128), f32))
    sums_t[me] = jnp.sum(mine, axis=0, keepdims=True)

    def pack(source, target, k):
        @pl.loop(0, n_tensor, unroll=4)
        def _(p):
            target[k, p] = source[jnp.maximum(chosen[k, p], 0)]

    def strip_of(p):
        return pl.ds(pl.multiple_of(p * strip, strip), strip)

    def scatter(source, target, k, number):
        @pl.loop(1, n_tensor)
        def _(i):
            dx = i // columns
            j = lax.rem(i, columns)
            odd = lax.rem(j, 2)
            dy = odd * ((j + 1) // 2) + (1 - odd) * lax.rem(columns - j // 2, columns)
            p = lax.rem(my_x + dx, n_tensor // columns) * columns + lax.rem(my_y + dy, columns)
            pltpu.make_async_remote_copy(
                src_ref=source.at[k, p],
                dst_ref=target.at[k, strip_of(me)],
                send_sem=send_sem.at[number],
                recv_sem=recv_sem.at[number],
                device_id={"tensor": p},
                device_id_type=MESH,
            ).start()

    def waiter(ref, number):
        return pltpu.make_async_remote_copy(
            src_ref=ref,
            dst_ref=ref,
            send_sem=send_sem.at[number],
            recv_sem=recv_sem.at[number],
            device_id={"tensor": lax.rem(me + 1, n_tensor)},
            device_id_type=MESH,
        )

    others = pl.ds(0, (n_tensor - 1) * strip)

    def send_sum(source, target, number, peer):
        pltpu.make_async_remote_copy(
            src_ref=source,
            dst_ref=target,
            send_sem=send_sem.at[number],
            recv_sem=recv_sem.at[number],
            device_id=peer,
            device_id_type=MESH,
        ).start()

    sum_of_t = sums_t.at[pl.ds(0, n_tensor - 1)]
    sum_of_d = sums_d.at[pl.ds(0, n_dp - 1)]

    @pl.when(me == lead)
    def _():
        pl.semaphore_wait(barrier, n_tensor + n_dp - 2)
        waiter(sum_of_t, 0).wait_recv()
        sums_d[group] = jnp.sum(sums_t[...], axis=0)

        @pl.loop(1, n_dp)
        def _(i):
            peer = {"dp": lax.rem(group + i, n_dp)}
            send_sum(sums_d.at[group], sums_d.at[group], 1, peer)

        waiter(sum_of_d, 1).wait_recv()
        total[...] = jnp.sum(sums_d[...], axis=0)

        @pl.loop(1, n_tensor)
        def _(i):
            send_sum(total, total, 8, {"tensor": lax.rem(lead + i, n_tensor)})

    @pl.when(me != lead)
    def _():
        pl.semaphore_wait(barrier, n_tensor - 1)
        send_sum(sums_t.at[me], sums_t.at[me], 0, {"tensor": lead})

    load_c.wait()
    for k in range(2):
        pack(grad_v, out_g, k)
        scatter(out_g, in_g, k, 2 + k)
        in_g[k, strip_of(me)] = out_g[k, me]
    load_l.wait()
    load_r.wait()
    for k in range(2):
        left_t[k] = left_v[k].T
        right_t[k] = right_v[k].T
    load_m.wait()

    @pl.when(me != lead)
    def _():
        waiter(total, 8).wait_recv()

    squared_sum = jnp.sum(total[...], keepdims=True)
    limit = clip_norm * clip_norm
    factor = jnp.where(
        squared_sum > limit, clip_norm / jnp.sqrt(jnp.maximum(squared_sum, limit)), 1.0
    )

    @pl.loop(0, blocks)
    def _(b):
        clipped = grad_v[b].astype(f32) * factor
        moved = momentum_decay * mom_v[b] + (1.0 - momentum_decay) * clipped
        mom_v[b] = moved
        moment_v[b] = moved.astype(bf16)

    store_m = pltpu.make_async_copy(mom_v, new_momentum, local_sem.at[1])
    store_m.start()
    for k in range(2):
        pack(moment_v, out_m, k)
        scatter(out_m, in_m, k, 4 + k)
        in_m[k, strip_of(me)] = out_m[k, me]

    share = factor * factor * ((1.0 - second_decay) / size)
    for k in range(2):
        waiter(in_g.at[k, others], 2 + k).wait_recv()
        half = dot(left_t[k], in_g[k]).astype(bf16)
        rotated = dot(half, right_v[k])
        square = rotated * rotated
        rows_old = row_stats[k : k + 1, :]
        cols_old = col_stats[k : k + 1, :]
        rows_next = second_decay * to_column(rows_old) + share * jnp.sum(
            square, axis=1, keepdims=True
        )
        cols_next = second_decay * cols_old + share * jnp.sum(square, axis=0, keepdims=True)
        mean = jnp.sum(rows_next, axis=0, keepdims=True) * (1.0 / size)
        inverse[k] = 1.0 / (jnp.sqrt(rows_next / mean) * jnp.sqrt(cols_next) + epsilon)
        used = jnp.full((1, size), chosen[k, me], jnp.int32) >= 0
        new_rows[k : k + 1, :] = jnp.where(used, to_row(rows_next), rows_old)
        new_cols[k : k + 1, :] = jnp.where(used, cols_next, cols_old)

    for k in range(2):
        waiter(in_m.at[k, others], 4 + k).wait_recv()
        half = dot(left_t[k], in_m[k]).astype(bf16)
        direction = (dot(half, right_v[k]) * inverse[k]).astype(bf16)
        for j in range(n_tensor // columns):
            c = lax.rem(my_x + j, n_tensor // columns)
            band = pl.ds(pl.multiple_of(c * chunk, chunk), chunk)
            half_back = dot(left_v[k, band], direction).astype(bf16)
            out_u[k, band] = dot(half_back, right_t[k]).astype(bf16)

            @pl.loop(1 if j == 0 else 0, columns)
            def _(i):
                p = c * columns + lax.rem(my_y + i, columns)
                pltpu.make_async_remote_copy(
                    src_ref=out_u.at[k, strip_of(p)],
                    dst_ref=in_u.at[k, me],
                    send_sem=send_sem.at[6 + k],
                    recv_sem=recv_sem.at[6 + k],
                    device_id={"tensor": p},
                    device_id_type=MESH,
                ).start()

        in_u[k, me] = out_u[k, strip_of(me)]

    for k in range(2):
        waiter(in_u.at[k, pl.ds(0, n_tensor - 1)], 6 + k).wait_recv()

    @pl.loop(0, blocks)
    def _(b):
        o = owners[0, b]
        rank = (chosen[0, o] != b).astype(jnp.int32)
        update_v[b] = in_u[rank, o]

    store_u = pltpu.make_async_copy(update_v, update, local_sem.at[0])
    store_u.start()

    @pl.when(me == lead)
    def _():
        waiter(sum_of_d, 1).wait_send()
        waiter(sum_of_t, 8).wait_send()

    @pl.when(me != lead)
    def _():
        waiter(total, 0).wait_send()

    for k in range(2):
        waiter(in_g.at[k, others], 2 + k).wait_send()
        waiter(in_m.at[k, others], 4 + k).wait_send()
        waiter(in_u.at[k, pl.ds(0, n_tensor - 1)], 6 + k).wait_send()
    store_m.wait()
    store_u.wait()


def store(*refs):
    copies = [
        pltpu.make_async_copy(refs[i], refs[4 + i], refs[8].at[i]) for i in range(4)
    ]
    for copy in copies:
        copy.start()
    for copy in copies:
        copy.wait()


def in_hbm(x):
    return pltpu.with_memory_space_constraint(x, pltpu.HBM)


def local(n_dp, n_tensor, gradient, momentum, eig_left, eig_right, row_stats, col_stats, owners):
    blocks, strip, size = gradient.shape
    slots = eig_left.shape[0]
    clip_norm = clip_share * size * math.sqrt(blocks * n_dp)
    anywhere = pl.BlockSpec(memory_space=pl.ANY)
    hbm = pl.BlockSpec(memory_space=pltpu.HBM)
    vmem = pl.BlockSpec(memory_space=pltpu.VMEM)
    square = (slots, size, size)
    pieces = (slots, n_tensor, strip, size)
    shapes = (
        jax.ShapeDtypeStruct(momentum.shape, f32),
        jax.ShapeDtypeStruct(gradient.shape, bf16),
        jax.ShapeDtypeStruct(row_stats.shape, f32),
        jax.ShapeDtypeStruct(col_stats.shape, f32),
    )
    arguments = (owners.reshape(1, blocks), gradient, momentum)
    arguments += (eig_left, eig_right, row_stats, col_stats)
    results = pl.pallas_call(
        functools.partial(kernel, n_dp, n_tensor, clip_norm),
        out_shape=shapes,
        in_specs=[
            pl.BlockSpec(memory_space=pltpu.SMEM),
            hbm,
            hbm,
            hbm,
            hbm,
            vmem,
            vmem,
        ],
        out_specs=(anywhere, anywhere, vmem, vmem),
        scratch_shapes=[
            pltpu.VMEM(gradient.shape, bf16),
            pltpu.VMEM(gradient.shape, f32),
            pltpu.VMEM(gradient.shape, bf16),
            pltpu.VMEM(gradient.shape, bf16),
            pltpu.VMEM(square, bf16),
            pltpu.VMEM(square, bf16),
            pltpu.VMEM(square, bf16),
            pltpu.VMEM(square, bf16),
            pltpu.VMEM(square, f32),
            pltpu.VMEM(pieces, bf16),
            pltpu.VMEM(pieces, bf16),
            pltpu.VMEM(square, bf16),
            pltpu.VMEM(square, bf16),
            pltpu.VMEM(square, bf16),
            pltpu.VMEM(pieces, bf16),
            pltpu.VMEM((n_tensor, 1, 128), f32),
            pltpu.VMEM((n_dp, 1, 128), f32),
            pltpu.VMEM((1, 128), f32),
            pltpu.VMEM((8, 128), jnp.int32),
            pltpu.SMEM((8, 128), jnp.int32),
            pltpu.SemaphoreType.DMA((5,)),
            pltpu.SemaphoreType.DMA((9,)),
            pltpu.SemaphoreType.DMA((9,)),
        ],
        compiler_params=pltpu.CompilerParams(
            collective_id=0, has_side_effects=True, vmem_limit_bytes=48 << 20
        ),
        name="soap_step",
    )(*map(in_hbm, arguments))
    return pl.pallas_call(
        store,
        out_shape=shapes,
        in_specs=[anywhere] * 4,
        out_specs=(hbm,) * 4,
        scratch_shapes=[pltpu.SemaphoreType.DMA((4,))],
        compiler_params=pltpu.CompilerParams(vmem_limit_bytes=48 << 20),
        name="store",
    )(*results)


def solution(mesh):
    placed = (
        P("dp", "tensor", None),
        P("dp", "tensor", None),
        P(("dp", "tensor"), None, None),
        P(("dp", "tensor"), None, None),
        P(("dp", "tensor"), None),
        P(("dp", "tensor"), None),
        P("dp", None),
    )
    return jax.shard_map(
        functools.partial(local, mesh.shape["dp"], mesh.shape["tensor"]),
        mesh=mesh,
        in_specs=placed,
        out_specs=(
            P("dp", "tensor", None),
            P("dp", "tensor", None),
            P(("dp", "tensor"), None),
            P(("dp", "tensor"), None),
        ),
        check_vma=False,
    )
```

```python
import functools
import math

import jax
import jax.numpy as jnp
from jax import lax
from jax.experimental import pallas as pl
from jax.experimental.pallas import tpu as pltpu
from jax.sharding import PartitionSpec as P

momentum_decay = 0.9
second_decay = 0.95
epsilon = 1e-08
clip_share = 0.25
columns = 8
lead = 11
extra = 4
chunk = 128
MESH = pl.DeviceIdType.MESH
f32 = jnp.float32
bf16 = jnp.bfloat16


def dot(a, b):
    return jnp.dot(a, b, preferred_element_type=f32)


def to_column(row):
    return jnp.broadcast_to(row, (128, row.shape[1])).T[:, 0:1]


def to_row(column):
    return jnp.broadcast_to(column, (column.shape[0], 128)).T[0:1, :]


def kernel(
    n_dp,
    n_tensor,
    clip_norm,
    owners,
    gradient,
    momentum,
    left,
    right,
    row_stats,
    col_stats,
    new_momentum,
    update,
    new_rows,
    new_cols,
    flags,
    grad_v,
    mom_v,
    moment_v,
    update_v,
    left_v,
    right_v,
    left_t,
    right_t,
    inverse,
    out_g,
    out_m,
    out_u,
    in_g,
    in_m,
    in_u,
    ring_g,
    ring_m,
    band_g,
    band_m,
    sums_t,
    sums_d,
    total,
    chosen_v,
    chosen,
    local_sem,
    send_sem,
    recv_sem,
    ring_send_sem,
    ring_recv_sem,
):
    blocks, strip, size = grad_v.shape
    me = lax.axis_index("tensor")
    group = lax.axis_index("dp")
    rows = n_tensor // columns
    my_x = me // columns
    my_y = lax.rem(me, columns)
    barrier = pltpu.get_barrier_semaphore()

    @pl.loop(1, n_tensor)
    def _(i):
        pl.semaphore_signal(
            barrier, inc=1, device_id={"tensor": lax.rem(me + i, n_tensor)}, device_id_type=MESH
        )

    @pl.when(me == lead)
    def _():
        @pl.loop(1, n_dp)
        def _(i):
            pl.semaphore_signal(
                barrier, inc=1, device_id={"dp": lax.rem(group + i, n_dp)}, device_id_type=MESH
            )

    load_g = pltpu.make_async_copy(gradient, grad_v, local_sem.at[0])
    load_m = pltpu.make_async_copy(momentum, mom_v, local_sem.at[1])
    load_l = pltpu.make_async_copy(left, left_v, local_sem.at[2])
    load_r = pltpu.make_async_copy(right, right_v, local_sem.at[3])
    load_g.start()
    load_m.start()
    load_l.start()
    load_r.start()

    lane = lax.broadcasted_iota(jnp.int32, (8, 128), 1)
    level = lax.broadcasted_iota(jnp.int32, (8, 128), 0)
    first = jnp.full((8, 128), -1, jnp.int32)
    second = first
    for b in range(blocks):
        mine = lane == owners[0, b]
        second = jnp.where(mine & (first >= 0), b, second)
        first = jnp.where(mine & (first < 0), b, first)
    double = (second >= 0).astype(jnp.int32)
    number = double
    for shift in (1, 2, 4, 8, 16):
        number = number + jnp.where(lane >= shift, pltpu.roll(number, shift, 1), 0)
    number = number - double
    listed = jnp.zeros((8, 128), jnp.int32)
    for j in range(extra):
        found = jnp.where((double > 0) & (number == j), second, 0)
        listed = jnp.where(lane == j, jnp.sum(found, axis=1, keepdims=True), listed)
    crowded = jnp.sum(double, axis=1, keepdims=True) > extra
    chosen_v[...] = jnp.where(
        level == 0,
        first,
        jnp.where(
            level == 1, second, jnp.where(level == 2, listed, jnp.minimum(number, extra - 1))
        ),
    )
    load_c = pltpu.make_async_copy(chosen_v, chosen, local_sem.at[4])
    load_c.start()
    load_g.wait()

    def squares(b, total):
        wide = grad_v[b].astype(f32)
        wide = wide * wide
        for j in range(size // 128):
            for i in range(strip // 8):
                total = total + wide[8 * i : 8 * i + 8, 128 * j : 128 * j + 128]
        return total

    part = lax.fori_loop(0, blocks, squares, jnp.zeros((8, 128), f32))
    part = jnp.sum(part + pltpu.roll(part, 64, 1), axis=0, keepdims=True)
    sums_t[me] = jnp.where(lane[0:1] < 64, part, crowded[0:1].astype(f32))

    def strip_of(p):
        return pl.ds(pl.multiple_of(p * strip, strip), strip)

    def band_of(c):
        return pl.ds(pl.multiple_of(c * chunk, chunk), chunk)

    def turned(i):
        return lax.rem(my_y + i + columns, columns)

    def exchange(source, outgoing, ring, band, target, phase, meanwhile):
        def start(src, dst, send, recv, peer):
            pltpu.make_async_remote_copy(
                src_ref=src,
                dst_ref=dst,
                send_sem=send,
                recv_sem=recv,
                device_id={"tensor": peer},
                device_id_type=MESH,
            ).start()

        def shares(hop):
            whole = pl.ds(0, extra)
            low, high = pl.ds(0, extra // 2), pl.ds(extra // 2, extra // 2)
            return (whole, whole) if hop < columns // 2 else (low, high)

        def pass_on(hop):
            for way, share in zip((1, -1), shares(hop)):
                entry = ring.at[turned(-way * (hop - 1)), share]
                start(
                    entry,
                    entry,
                    ring_send_sem.at[phase],
                    ring_recv_sem.at[phase, 2 * hop - 2 + (way < 0)],
                    my_x * columns + turned(way),
                )

        def arrive(hop):
            for way, share in zip((1, -1), shares(hop)):
                entry = ring.at[turned(-way * hop), share]
                pltpu.make_async_remote_copy(
                    src_ref=entry,
                    dst_ref=entry,
                    send_sem=ring_send_sem.at[phase],
                    recv_sem=ring_recv_sem.at[phase, 2 * hop - 2 + (way < 0)],
                    device_id={"tensor": my_x * columns + turned(way)},
                    device_id_type=MESH,
                ).wait_recv()

        def scatter(dx):
            row = lax.rem(my_x + dx, rows) * columns

            @pl.loop(1 if dx == 0 else 0, columns)
            def _(i):
                odd = lax.rem(i, 2)
                p = row + turned(odd * ((i + 1) // 2) - (1 - odd) * (i // 2))
                outgoing[p] = source[jnp.maximum(chosen[0, p], 0)]
                start(
                    outgoing.at[p],
                    target.at[0, strip_of(me)],
                    send_sem.at[2 + 2 * phase],
                    recv_sem.at[2 + 2 * phase],
                    p,
                )

        for j in range(extra):
            ring[my_y, j] = source[chosen[2, j]]
        pass_on(1)
        target[0, strip_of(me)] = source[jnp.maximum(chosen[0, me], 0)]
        scatter(0)
        for hop in range(1, columns // 2):
            scatter(hop)
            arrive(hop)
            pass_on(hop + 1)
            if hop in meanwhile:
                meanwhile[hop]()
        arrive(columns // 2)
        for c in range(rows):
            j = chosen[3, c * columns + my_y]
            for y in range(columns):
                band[c, strip * y : strip * (y + 1)] = ring[y, j]
        target[1, band_of(my_x)] = band[my_x]
        for i in range(1, rows):
            c = lax.rem(my_x + i, rows)
            start(
                band.at[c],
                target.at[1, band_of(my_x)],
                send_sem.at[3 + 2 * phase],
                recv_sem.at[3 + 2 * phase],
                c * columns + my_y,
            )

    def waiter(ref, number):
        return pltpu.make_async_remote_copy(
            src_ref=ref,
            dst_ref=ref,
            send_sem=send_sem.at[number],
            recv_sem=recv_sem.at[number],
            device_id={"tensor": lax.rem(me + 1, n_tensor)},
            device_id_type=MESH,
        )

    others = (pl.ds(0, (n_tensor - 1) * strip), pl.ds(0, (rows - 1) * chunk))

    def send_sum(source, target, number, peer):
        pltpu.make_async_remote_copy(
            src_ref=source,
            dst_ref=target,
            send_sem=send_sem.at[number],
            recv_sem=recv_sem.at[number],
            device_id=peer,
            device_id_type=MESH,
        ).start()

    sum_of_t = sums_t.at[pl.ds(0, n_tensor - 1)]
    sum_of_d = sums_d.at[pl.ds(0, n_dp - 1)]

    @pl.when(me == lead)
    def _():
        pl.semaphore_wait(barrier, n_tensor + n_dp - 2)
        waiter(sum_of_t, 0).wait_recv()
        sums_d[group] = jnp.sum(sums_t[...], axis=0)

        @pl.loop(1, n_dp)
        def _(i):
            peer = {"dp": lax.rem(group + i, n_dp)}
            send_sum(sums_d.at[group], sums_d.at[group], 1, peer)

    @pl.when(me != lead)
    def _():
        pl.semaphore_wait(barrier, n_tensor - 1)
        send_sum(sums_t.at[me], sums_t.at[me], 0, {"tensor": lead})

    load_c.wait()
    def announce():
        @pl.when(me == lead)
        def _():
            waiter(sum_of_d, 1).wait_recv()
            total[...] = jnp.sum(sums_d[...], axis=0)

            @pl.loop(1, n_tensor)
            def _(i):
                send_sum(total, total, 8, {"tensor": lax.rem(lead + i, n_tensor)})

    def transpose():
        load_l.wait()
        load_r.wait()
        for k in range(2):
            left_t[k] = left_v[k].T
            right_t[k] = right_v[k].T

    exchange(grad_v, out_g, ring_g, band_g, in_g, 0, {2: announce, 3: transpose})
    load_m.wait()

    @pl.when(me != lead)
    def _():
        waiter(total, 8).wait_recv()

    flags[...] = total[...]
    squared_sum = jnp.sum(jnp.where(lane[0:1] < 64, total[...], 0.0), keepdims=True)
    limit = clip_norm * clip_norm
    factor = jnp.where(
        squared_sum > limit, clip_norm / jnp.sqrt(jnp.maximum(squared_sum, limit)), 1.0
    )

    @pl.loop(0, blocks)
    def _(b):
        clipped = grad_v[b].astype(f32) * factor
        moved = momentum_decay * mom_v[b] + (1.0 - momentum_decay) * clipped
        mom_v[b] = moved
        moment_v[b] = moved.astype(bf16)

    store_m = pltpu.make_async_copy(mom_v, new_momentum, local_sem.at[1])
    store_m.start()
    share = factor * factor * ((1.0 - second_decay) / size)
    def statistics(k):
        waiter(in_g.at[k, others[k]], 2 + k).wait_recv()
        half = dot(left_t[k], in_g[k]).astype(bf16)
        rotated = dot(half, right_v[k])
        square = rotated * rotated
        rows_old = row_stats[k : k + 1, :]
        cols_old = col_stats[k : k + 1, :]
        rows_next = second_decay * to_column(rows_old) + share * jnp.sum(
            square, axis=1, keepdims=True
        )
        cols_next = second_decay * cols_old + share * jnp.sum(square, axis=0, keepdims=True)
        mean = jnp.sum(rows_next, axis=0, keepdims=True) * (1.0 / size)
        inverse[k] = 1.0 / (jnp.sqrt(rows_next / mean) * jnp.sqrt(cols_next) + epsilon)
        used = jnp.full((1, size), chosen[k, me], jnp.int32) >= 0
        new_rows[k : k + 1, :] = jnp.where(used, to_row(rows_next), rows_old)
        new_cols[k : k + 1, :] = jnp.where(used, cols_next, cols_old)

    exchange(
        moment_v,
        out_m,
        ring_m,
        band_m,
        in_m,
        1,
        {1: lambda: statistics(0), 3: lambda: statistics(1)},
    )


    for k in range(2):
        waiter(in_m.at[k, others[k]], 4 + k).wait_recv()
        half = dot(left_t[k], in_m[k]).astype(bf16)
        direction = (dot(half, right_v[k]) * inverse[k]).astype(bf16)
        for j in range(n_tensor // columns):
            c = lax.rem(my_x + j, n_tensor // columns)
            band = band_of(c)
            half_back = dot(left_v[k, band], direction).astype(bf16)
            out_u[k, band] = dot(half_back, right_t[k]).astype(bf16)

            @pl.loop(1 if j == 0 else 0, columns)
            def _(i):
                p = c * columns + lax.rem(my_y + i, columns)
                pltpu.make_async_remote_copy(
                    src_ref=out_u.at[k, strip_of(p)],
                    dst_ref=in_u.at[k, me],
                    send_sem=send_sem.at[6 + k],
                    recv_sem=recv_sem.at[6 + k],
                    device_id={"tensor": p},
                    device_id_type=MESH,
                ).start()

        in_u[k, me] = out_u[k, strip_of(me)]

    for k in range(2):
        waiter(in_u.at[k, pl.ds(0, n_tensor - 1)], 6 + k).wait_recv()

    @pl.loop(0, blocks)
    def _(b):
        o = owners[0, b]
        rank = (chosen[0, o] != b).astype(jnp.int32)
        update_v[b] = in_u[rank, o]

    store_u = pltpu.make_async_copy(update_v, update, local_sem.at[0])
    store_u.start()

    @pl.when(me == lead)
    def _():
        waiter(sum_of_d, 1).wait_send()
        waiter(sum_of_t, 8).wait_send()

    @pl.when(me != lead)
    def _():
        waiter(total, 0).wait_send()

    for k in range(2):
        waiter(in_g.at[k, others[k]], 2 + k).wait_send()
        waiter(in_m.at[k, others[k]], 4 + k).wait_send()
        waiter(in_u.at[k, pl.ds(0, n_tensor - 1)], 6 + k).wait_send()
    for ring, phase in ((ring_g, 0), (ring_m, 1)):
        sent = ring.at[pl.ds(0, columns - 1)]
        pltpu.make_async_remote_copy(
            src_ref=sent,
            dst_ref=sent,
            send_sem=ring_send_sem.at[phase],
            recv_sem=ring_recv_sem.at[phase, 0],
            device_id={"tensor": lax.rem(me + 1, n_tensor)},
            device_id_type=MESH,
        ).wait_send()
    store_m.wait()
    store_u.wait()


def store(*refs):
    copies = [
        pltpu.make_async_copy(refs[i], refs[4 + i], refs[8].at[i]) for i in range(4)
    ]
    for copy in copies:
        copy.start()
    for copy in copies:
        copy.wait()


def precondition(arrived, left_basis, right_basis, row_stats, col_stats, in_use):
    halves = jnp.einsum(
        "kij,kcil->kcjl", left_basis, arrived, preferred_element_type=jnp.float32
    ).astype(jnp.bfloat16)
    rotated = jnp.einsum("kcjl,klm->kcjm", halves, right_basis, preferred_element_type=jnp.float32)
    rot_grad = rotated[:, 0]
    rot_moment = rotated[:, 1]
    squares = rot_grad * rot_grad
    rows_next = second_decay * row_stats + (1.0 - second_decay) * jnp.mean(squares, axis=2)
    cols_next = second_decay * col_stats + (1.0 - second_decay) * jnp.mean(squares, axis=1)
    scale_hat = (
        rows_next[:, :, None] * cols_next[:, None, :] / jnp.mean(rows_next, axis=1)[:, None, None]
    )
    direction = (rot_moment / (jnp.sqrt(scale_hat) + epsilon)).astype(jnp.bfloat16)
    half_back = jnp.einsum(
        "kij,kjl->kil", left_basis, direction, preferred_element_type=jnp.float32
    ).astype(jnp.bfloat16)
    finished = jnp.einsum(
        "kil,kml->kim", half_back, right_basis, preferred_element_type=jnp.float32
    ).astype(jnp.bfloat16)
    kept_rows = jnp.where(in_use[:, None], rows_next, row_stats)
    kept_cols = jnp.where(in_use[:, None], cols_next, col_stats)
    return (finished, kept_rows, kept_cols)


def general(gradient, momentum, eig_left, eig_right, row_stats, col_stats, owners):
    group_blocks, strip_rows, block_size = gradient.shape
    owner_slots = eig_left.shape[0]
    tensor_size = lax.axis_size("tensor")
    whole_blocks = group_blocks * lax.axis_size("dp")
    widened = gradient.astype(jnp.float32)
    squared_sum = lax.psum(jnp.sum(widened * widened), ("dp", "tensor"))
    factor = jnp.minimum(
        1.0, clip_share * block_size * math.sqrt(whole_blocks) / jnp.sqrt(squared_sum)
    )
    clipped = widened * factor
    new_momentum = momentum_decay * momentum + (1.0 - momentum_decay) * clipped
    payload = jnp.stack([clipped.astype(jnp.bfloat16), new_momentum.astype(jnp.bfloat16)], axis=1)
    payload = payload.reshape(group_blocks, 2, strip_rows * block_size)
    holders = owners[:, 0]
    counter = jnp.arange(group_blocks, dtype=jnp.int32)
    same_owner = holders[:, None] == holders[None, :]
    before = counter[None, :] < counter[:, None]
    earlier_count = jnp.sum((same_owner & before).astype(jnp.int32), axis=1)
    slot_match = (
        earlier_count[None, None, :] == jnp.arange(owner_slots, dtype=jnp.int32)[:, None, None]
    )
    owner_match = holders[None, None, :] == jnp.arange(tensor_size, dtype=jnp.int32)[None, :, None]
    selector = (slot_match & owner_match).astype(jnp.bfloat16)
    outgoing = jnp.einsum(
        "kpb,bcx->kcpx", selector, payload, preferred_element_type=jnp.float32
    ).astype(jnp.bfloat16)
    owned_count = jnp.sum((holders == lax.axis_index("tensor")).astype(jnp.int32))
    in_use = jnp.arange(owner_slots, dtype=jnp.int32) < owned_count
    arrived = lax.all_to_all(outgoing, "tensor", split_axis=2, concat_axis=2, tiled=True)
    arrived = arrived.reshape(owner_slots, 2, block_size, block_size)
    finished, new_rows, new_cols = precondition(
        arrived, eig_left, eig_right, row_stats, col_stats, in_use
    )
    returned = lax.all_to_all(
        finished.reshape(owner_slots, tensor_size, strip_rows * block_size),
        "tensor",
        split_axis=1,
        concat_axis=1,
        tiled=True,
    )
    update = jnp.einsum(
        "kpb,kpx->bx", selector, returned, preferred_element_type=jnp.float32
    ).astype(jnp.bfloat16)
    update = update.reshape(group_blocks, strip_rows, block_size)
    return (new_momentum, update, new_rows, new_cols)


def in_hbm(x):
    return pltpu.with_memory_space_constraint(x, pltpu.HBM)


def local(n_dp, n_tensor, gradient, momentum, eig_left, eig_right, row_stats, col_stats, owners):
    blocks, strip, size = gradient.shape
    slots = eig_left.shape[0]
    clip_norm = clip_share * size * math.sqrt(blocks * n_dp)
    anywhere = pl.BlockSpec(memory_space=pl.ANY)
    hbm = pl.BlockSpec(memory_space=pltpu.HBM)
    vmem = pl.BlockSpec(memory_space=pltpu.VMEM)
    square = (slots, size, size)
    pieces = (n_tensor, strip, size)
    ring = (columns, extra, strip, size)
    bands = (n_tensor // columns, chunk, size)
    shapes = (
        jax.ShapeDtypeStruct(momentum.shape, f32),
        jax.ShapeDtypeStruct(gradient.shape, bf16),
        jax.ShapeDtypeStruct(row_stats.shape, f32),
        jax.ShapeDtypeStruct(col_stats.shape, f32),
    )
    arguments = (owners.reshape(1, blocks), gradient, momentum)
    arguments += (eig_left, eig_right, row_stats, col_stats)
    *results, flags = pl.pallas_call(
        functools.partial(kernel, n_dp, n_tensor, clip_norm),
        out_shape=(*shapes, jax.ShapeDtypeStruct((1, 128), f32)),
        in_specs=[
            pl.BlockSpec(memory_space=pltpu.SMEM),
            hbm,
            hbm,
            hbm,
            hbm,
            vmem,
            vmem,
        ],
        out_specs=(anywhere, anywhere, vmem, vmem, vmem),
        scratch_shapes=[
            pltpu.VMEM(gradient.shape, bf16),
            pltpu.VMEM(gradient.shape, f32),
            pltpu.VMEM(gradient.shape, bf16),
            pltpu.VMEM(gradient.shape, bf16),
            pltpu.VMEM(square, bf16),
            pltpu.VMEM(square, bf16),
            pltpu.VMEM(square, bf16),
            pltpu.VMEM(square, bf16),
            pltpu.VMEM(square, f32),
            pltpu.VMEM(pieces, bf16),
            pltpu.VMEM(pieces, bf16),
            pltpu.VMEM(square, bf16),
            pltpu.VMEM(square, bf16),
            pltpu.VMEM(square, bf16),
            pltpu.VMEM((slots, *pieces), bf16),
            pltpu.VMEM(ring, bf16),
            pltpu.VMEM(ring, bf16),
            pltpu.VMEM(bands, bf16),
            pltpu.VMEM(bands, bf16),
            pltpu.VMEM((n_tensor, 1, 128), f32),
            pltpu.VMEM((n_dp, 1, 128), f32),
            pltpu.VMEM((1, 128), f32),
            pltpu.VMEM((8, 128), jnp.int32),
            pltpu.SMEM((8, 128), jnp.int32),
            pltpu.SemaphoreType.DMA((5,)),
            pltpu.SemaphoreType.DMA((9,)),
            pltpu.SemaphoreType.DMA((9,)),
            pltpu.SemaphoreType.DMA((2,)),
            pltpu.SemaphoreType.DMA((2, columns)),
        ],
        compiler_params=pltpu.CompilerParams(
            collective_id=0, has_side_effects=True, vmem_limit_bytes=48 << 20
        ),
        name="soap_step",
    )(*map(in_hbm, arguments))
    keep = pl.pallas_call(
        store,
        out_shape=shapes,
        in_specs=[anywhere] * 4,
        out_specs=(hbm,) * 4,
        scratch_shapes=[pltpu.SemaphoreType.DMA((4,))],
        compiler_params=pltpu.CompilerParams(vmem_limit_bytes=48 << 20),
        name="store",
    )
    inputs = (gradient, momentum, eig_left, eig_right, row_stats, col_stats, owners)
    return lax.cond(
        flags[0, 127] > 0.5,
        lambda done, given: tuple(general(*given)),
        lambda done, given: tuple(keep(*done)),
        tuple(results),
        inputs,
    )


def solution(mesh):
    placed = (
        P("dp", "tensor", None),
        P("dp", "tensor", None),
        P(("dp", "tensor"), None, None),
        P(("dp", "tensor"), None, None),
        P(("dp", "tensor"), None),
        P(("dp", "tensor"), None),
        P("dp", None),
    )
    return jax.shard_map(
        functools.partial(local, mesh.shape["dp"], mesh.shape["tensor"]),
        mesh=mesh,
        in_specs=placed,
        out_specs=(
            P("dp", "tensor", None),
            P("dp", "tensor", None),
            P(("dp", "tensor"), None),
            P(("dp", "tensor"), None),
        ),
        check_vma=False,
    )
```

```python
import functools
import math

import jax
import jax.numpy as jnp
from jax import lax
from jax.experimental import pallas as pl
from jax.experimental.pallas import tpu as pltpu
from jax.sharding import PartitionSpec as P

momentum_decay = 0.9
second_decay = 0.95
epsilon = 1e-08
clip_share = 0.25
columns = 8
lead = 11
extra = 4
chunk = 128
MESH = pl.DeviceIdType.MESH
f32 = jnp.float32
bf16 = jnp.bfloat16


def dot(a, b):
    return jnp.dot(a, b, preferred_element_type=f32)


def to_column(row):
    return jnp.broadcast_to(row, (128, row.shape[1])).T[:, 0:1]


def to_row(column):
    return jnp.broadcast_to(column, (column.shape[0], 128)).T[0:1, :]


def kernel(
    n_dp,
    n_tensor,
    clip_norm,
    owners,
    gradient,
    momentum,
    left,
    right,
    row_stats,
    col_stats,
    new_momentum,
    update,
    new_rows,
    new_cols,
    flags,
    grad_v,
    mom_v,
    moment_v,
    update_v,
    left_v,
    right_v,
    left_t,
    right_t,
    inverse,
    out_g,
    out_m,
    out_u,
    in_g,
    in_m,
    in_u,
    ring_g,
    ring_m,
    band_g,
    band_m,
    sums_t,
    sums_d,
    total,
    chosen_v,
    chosen,
    local_sem,
    send_sem,
    recv_sem,
    ring_send_sem,
    ring_recv_sem,
):
    blocks, strip, size = grad_v.shape
    me = lax.axis_index("tensor")
    group = lax.axis_index("dp")
    rows = n_tensor // columns
    my_x = me // columns
    my_y = lax.rem(me, columns)
    barrier = pltpu.get_barrier_semaphore()

    @pl.loop(1, n_tensor)
    def _(i):
        pl.semaphore_signal(
            barrier, inc=1, device_id={"tensor": lax.rem(me + i, n_tensor)}, device_id_type=MESH
        )

    @pl.when(me == lead)
    def _():
        @pl.loop(1, n_dp)
        def _(i):
            pl.semaphore_signal(
                barrier, inc=1, device_id={"dp": lax.rem(group + i, n_dp)}, device_id_type=MESH
            )

    load_g = pltpu.make_async_copy(gradient, grad_v, local_sem.at[0])
    load_m = pltpu.make_async_copy(momentum, mom_v, local_sem.at[1])
    load_l = pltpu.make_async_copy(left, left_v, local_sem.at[2])
    load_r = pltpu.make_async_copy(right, right_v, local_sem.at[3])
    load_g.start()
    load_m.start()
    load_l.start()
    load_r.start()

    lane = lax.broadcasted_iota(jnp.int32, (8, 128), 1)
    level = lax.broadcasted_iota(jnp.int32, (8, 128), 0)
    first = jnp.full((8, 128), -1, jnp.int32)
    second = first
    for b in range(blocks):
        mine = lane == owners[0, b]
        second = jnp.where(mine & (first >= 0), b, second)
        first = jnp.where(mine & (first < 0), b, first)
    double = (second >= 0).astype(jnp.int32)
    number = double
    for shift in (1, 2, 4, 8, 16):
        number = number + jnp.where(lane >= shift, pltpu.roll(number, shift, 1), 0)
    number = number - double
    listed = jnp.zeros((8, 128), jnp.int32)
    for j in range(extra):
        found = jnp.where((double > 0) & (number == j), second, 0)
        listed = jnp.where(lane == j, jnp.sum(found, axis=1, keepdims=True), listed)
    crowded = jnp.sum(double, axis=1, keepdims=True) > extra
    chosen_v[...] = jnp.where(
        level == 0,
        first,
        jnp.where(
            level == 1, second, jnp.where(level == 2, listed, jnp.minimum(number, extra - 1))
        ),
    )
    load_c = pltpu.make_async_copy(chosen_v, chosen, local_sem.at[4])
    load_c.start()
    load_g.wait()

    def squares(b, total):
        wide = grad_v[b].astype(f32)
        wide = wide * wide
        for j in range(size // 128):
            for i in range(strip // 8):
                total = total + wide[8 * i : 8 * i + 8, 128 * j : 128 * j + 128]
        return total

    part = lax.fori_loop(0, blocks, squares, jnp.zeros((8, 128), f32))
    part = jnp.sum(part + pltpu.roll(part, 64, 1), axis=0, keepdims=True)
    sums_t[me] = jnp.where(lane[0:1] < 64, part, crowded[0:1].astype(f32))

    def strip_of(p):
        return pl.ds(pl.multiple_of(p * strip, strip), strip)

    def band_of(c):
        return pl.ds(pl.multiple_of(c * chunk, chunk), chunk)

    def turned(i):
        return lax.rem(my_y + i + columns, columns)

    def exchange(source, outgoing, ring, band, target, phase, meanwhile):
        def start(src, dst, send, recv, peer):
            pltpu.make_async_remote_copy(
                src_ref=src,
                dst_ref=dst,
                send_sem=send,
                recv_sem=recv,
                device_id={"tensor": peer},
                device_id_type=MESH,
            ).start()

        def shares(hop):
            whole = pl.ds(0, extra)
            low, high = pl.ds(0, extra // 2), pl.ds(extra // 2, extra // 2)
            return (whole, whole) if hop < columns // 2 else (low, high)

        def pass_on(hop):
            for way, share in zip((1, -1), shares(hop)):
                entry = ring.at[turned(-way * (hop - 1)), share]
                start(
                    entry,
                    entry,
                    ring_send_sem.at[phase],
                    ring_recv_sem.at[phase, 2 * hop - 2 + (way < 0)],
                    my_x * columns + turned(way),
                )

        def arrive(hop):
            for way, share in zip((1, -1), shares(hop)):
                entry = ring.at[turned(-way * hop), share]
                pltpu.make_async_remote_copy(
                    src_ref=entry,
                    dst_ref=entry,
                    send_sem=ring_send_sem.at[phase],
                    recv_sem=ring_recv_sem.at[phase, 2 * hop - 2 + (way < 0)],
                    device_id={"tensor": my_x * columns + turned(way)},
                    device_id_type=MESH,
                ).wait_recv()

        def scatter(dx):
            row = lax.rem(my_x + dx, rows) * columns

            @pl.loop(1 if dx == 0 else 0, columns)
            def _(i):
                odd = lax.rem(i, 2)
                p = row + turned(odd * ((i + 1) // 2) - (1 - odd) * (i // 2))
                outgoing[p] = source[jnp.maximum(chosen[0, p], 0)]
                start(
                    outgoing.at[p],
                    target.at[0, strip_of(me)],
                    send_sem.at[2 + 2 * phase],
                    recv_sem.at[2 + 2 * phase],
                    p,
                )

        for j in range(extra):
            ring[my_y, j] = source[chosen[2, j]]
        pass_on(1)
        target[0, strip_of(me)] = source[jnp.maximum(chosen[0, me], 0)]
        scatter(0)
        for hop in range(1, columns // 2):
            scatter(hop)
            arrive(hop)
            pass_on(hop + 1)
            if hop in meanwhile:
                meanwhile[hop]()
        arrive(columns // 2)
        for c in range(rows):
            j = chosen[3, c * columns + my_y]
            for y in range(columns):
                band[c, strip * y : strip * (y + 1)] = ring[y, j]
        target[1, band_of(my_x)] = band[my_x]
        for i in range(1, rows):
            c = lax.rem(my_x + i, rows)
            start(
                band.at[c],
                target.at[1, band_of(my_x)],
                send_sem.at[3 + 2 * phase],
                recv_sem.at[3 + 2 * phase],
                c * columns + my_y,
            )

    def waiter(ref, number):
        return pltpu.make_async_remote_copy(
            src_ref=ref,
            dst_ref=ref,
            send_sem=send_sem.at[number],
            recv_sem=recv_sem.at[number],
            device_id={"tensor": lax.rem(me + 1, n_tensor)},
            device_id_type=MESH,
        )

    others = (pl.ds(0, (n_tensor - 1) * strip), pl.ds(0, (rows - 1) * chunk))

    def send_sum(source, target, number, peer):
        pltpu.make_async_remote_copy(
            src_ref=source,
            dst_ref=target,
            send_sem=send_sem.at[number],
            recv_sem=recv_sem.at[number],
            device_id=peer,
            device_id_type=MESH,
        ).start()

    sum_of_t = sums_t.at[pl.ds(0, n_tensor - 1)]
    sum_of_d = sums_d.at[pl.ds(0, n_dp - 1)]

    @pl.when(me == lead)
    def _():
        pl.semaphore_wait(barrier, n_tensor + n_dp - 2)
        waiter(sum_of_t, 0).wait_recv()
        sums_d[group] = jnp.sum(sums_t[...], axis=0)

        @pl.loop(1, n_dp)
        def _(i):
            peer = {"dp": lax.rem(group + i, n_dp)}
            send_sum(sums_d.at[group], sums_d.at[group], 1, peer)

    @pl.when(me != lead)
    def _():
        pl.semaphore_wait(barrier, n_tensor - 1)
        send_sum(sums_t.at[me], sums_t.at[me], 0, {"tensor": lead})

    load_c.wait()
    def announce():
        @pl.when(me == lead)
        def _():
            waiter(sum_of_d, 1).wait_recv()
            total[...] = jnp.sum(sums_d[...], axis=0)

            @pl.loop(1, n_tensor)
            def _(i):
                send_sum(total, total, 8, {"tensor": lax.rem(lead + i, n_tensor)})

    def transpose():
        load_l.wait()
        load_r.wait()
        for k in range(2):
            left_t[k] = left_v[k].T
            right_t[k] = right_v[k].T

    exchange(grad_v, out_g, ring_g, band_g, in_g, 0, {2: announce, 3: transpose})
    load_m.wait()

    @pl.when(me != lead)
    def _():
        waiter(total, 8).wait_recv()

    flags[...] = total[...]
    squared_sum = jnp.sum(jnp.where(lane[0:1] < 64, total[...], 0.0), keepdims=True)
    limit = clip_norm * clip_norm
    factor = jnp.where(
        squared_sum > limit, clip_norm / jnp.sqrt(jnp.maximum(squared_sum, limit)), 1.0
    )

    @pl.loop(0, blocks)
    def _(b):
        clipped = grad_v[b].astype(f32) * factor
        moved = momentum_decay * mom_v[b] + (1.0 - momentum_decay) * clipped
        mom_v[b] = moved
        moment_v[b] = moved.astype(bf16)

    store_m = pltpu.make_async_copy(mom_v, new_momentum, local_sem.at[1])
    store_m.start()
    share = factor * factor * ((1.0 - second_decay) / size)
    def statistics(k):
        waiter(in_g.at[k, others[k]], 2 + k).wait_recv()
        half = dot(left_t[k], in_g[k]).astype(bf16)
        rotated = dot(half, right_v[k])
        square = rotated * rotated
        rows_old = row_stats[k : k + 1, :]
        cols_old = col_stats[k : k + 1, :]
        rows_next = second_decay * to_column(rows_old) + share * jnp.sum(
            square, axis=1, keepdims=True
        )
        cols_next = second_decay * cols_old + share * jnp.sum(square, axis=0, keepdims=True)
        mean = jnp.sum(rows_next, axis=0, keepdims=True) * (1.0 / size)
        inverse[k] = 1.0 / (jnp.sqrt(rows_next / mean) * jnp.sqrt(cols_next) + epsilon)
        used = jnp.full((1, size), chosen[k, me], jnp.int32) >= 0
        new_rows[k : k + 1, :] = jnp.where(used, to_row(rows_next), rows_old)
        new_cols[k : k + 1, :] = jnp.where(used, cols_next, cols_old)

    exchange(
        moment_v,
        out_m,
        ring_m,
        band_m,
        in_m,
        1,
        {1: lambda: statistics(0), 3: lambda: statistics(1)},
    )


    for k in range(2):
        waiter(in_m.at[k, others[k]], 4 + k).wait_recv()
        half = dot(left_t[k], in_m[k]).astype(bf16)
        direction = (dot(half, right_v[k]) * inverse[k]).astype(bf16)
        for j in range(n_tensor // columns):
            c = lax.rem(my_x + j, n_tensor // columns)
            band = band_of(c)
            half_back = dot(left_v[k, band], direction).astype(bf16)
            out_u[k, band] = dot(half_back, right_t[k]).astype(bf16)

            @pl.loop(1 if j == 0 else 0, columns)
            def _(i):
                p = c * columns + lax.rem(my_y + i, columns)
                pltpu.make_async_remote_copy(
                    src_ref=out_u.at[k, strip_of(p)],
                    dst_ref=in_u.at[k, me],
                    send_sem=send_sem.at[6 + k],
                    recv_sem=recv_sem.at[6 + k],
                    device_id={"tensor": p},
                    device_id_type=MESH,
                ).start()

        in_u[k, me] = out_u[k, strip_of(me)]

    for k in range(2):
        waiter(in_u.at[k, pl.ds(0, n_tensor - 1)], 6 + k).wait_recv()

    @pl.loop(0, blocks)
    def _(b):
        o = owners[0, b]
        rank = (chosen[0, o] != b).astype(jnp.int32)
        update_v[b] = in_u[rank, o]

    store_u = pltpu.make_async_copy(update_v, update, local_sem.at[0])
    store_u.start()

    @pl.when(me == lead)
    def _():
        waiter(sum_of_d, 1).wait_send()
        waiter(sum_of_t, 8).wait_send()

    @pl.when(me != lead)
    def _():
        waiter(total, 0).wait_send()

    for k in range(2):
        waiter(in_g.at[k, others[k]], 2 + k).wait_send()
        waiter(in_m.at[k, others[k]], 4 + k).wait_send()
        waiter(in_u.at[k, pl.ds(0, n_tensor - 1)], 6 + k).wait_send()
    for ring, phase in ((ring_g, 0), (ring_m, 1)):
        sent = ring.at[pl.ds(0, columns - 1)]
        pltpu.make_async_remote_copy(
            src_ref=sent,
            dst_ref=sent,
            send_sem=ring_send_sem.at[phase],
            recv_sem=ring_recv_sem.at[phase, 0],
            device_id={"tensor": lax.rem(me + 1, n_tensor)},
            device_id_type=MESH,
        ).wait_send()
    store_m.wait()
    store_u.wait()


def store(*refs):
    copies = [
        pltpu.make_async_copy(refs[i], refs[4 + i], refs[8].at[i]) for i in range(4)
    ]
    for copy in copies:
        copy.start()
    for copy in copies:
        copy.wait()


def precondition(arrived, left_basis, right_basis, row_stats, col_stats, in_use):
    halves = jnp.einsum(
        "kij,kcil->kcjl", left_basis, arrived, preferred_element_type=jnp.float32
    ).astype(jnp.bfloat16)
    rotated = jnp.einsum("kcjl,klm->kcjm", halves, right_basis, preferred_element_type=jnp.float32)
    rot_grad = rotated[:, 0]
    rot_moment = rotated[:, 1]
    squares = rot_grad * rot_grad
    rows_next = second_decay * row_stats + (1.0 - second_decay) * jnp.mean(squares, axis=2)
    cols_next = second_decay * col_stats + (1.0 - second_decay) * jnp.mean(squares, axis=1)
    scale_hat = (
        rows_next[:, :, None] * cols_next[:, None, :] / jnp.mean(rows_next, axis=1)[:, None, None]
    )
    direction = (rot_moment / (jnp.sqrt(scale_hat) + epsilon)).astype(jnp.bfloat16)
    half_back = jnp.einsum(
        "kij,kjl->kil", left_basis, direction, preferred_element_type=jnp.float32
    ).astype(jnp.bfloat16)
    finished = jnp.einsum(
        "kil,kml->kim", half_back, right_basis, preferred_element_type=jnp.float32
    ).astype(jnp.bfloat16)
    kept_rows = jnp.where(in_use[:, None], rows_next, row_stats)
    kept_cols = jnp.where(in_use[:, None], cols_next, col_stats)
    return (finished, kept_rows, kept_cols)


def general(gradient, momentum, eig_left, eig_right, row_stats, col_stats, owners):
    group_blocks, strip_rows, block_size = gradient.shape
    owner_slots = eig_left.shape[0]
    tensor_size = lax.axis_size("tensor")
    whole_blocks = group_blocks * lax.axis_size("dp")
    widened = gradient.astype(jnp.float32)
    squared_sum = lax.psum(jnp.sum(widened * widened), ("dp", "tensor"))
    factor = jnp.minimum(
        1.0, clip_share * block_size * math.sqrt(whole_blocks) / jnp.sqrt(squared_sum)
    )
    clipped = widened * factor
    new_momentum = momentum_decay * momentum + (1.0 - momentum_decay) * clipped
    payload = jnp.stack([clipped.astype(jnp.bfloat16), new_momentum.astype(jnp.bfloat16)], axis=1)
    payload = payload.reshape(group_blocks, 2, strip_rows * block_size)
    holders = owners[:, 0]
    counter = jnp.arange(group_blocks, dtype=jnp.int32)
    same_owner = holders[:, None] == holders[None, :]
    before = counter[None, :] < counter[:, None]
    earlier_count = jnp.sum((same_owner & before).astype(jnp.int32), axis=1)
    slot_match = (
        earlier_count[None, None, :] == jnp.arange(owner_slots, dtype=jnp.int32)[:, None, None]
    )
    owner_match = holders[None, None, :] == jnp.arange(tensor_size, dtype=jnp.int32)[None, :, None]
    selector = (slot_match & owner_match).astype(jnp.bfloat16)
    outgoing = jnp.einsum(
        "kpb,bcx->kcpx", selector, payload, preferred_element_type=jnp.float32
    ).astype(jnp.bfloat16)
    owned_count = jnp.sum((holders == lax.axis_index("tensor")).astype(jnp.int32))
    in_use = jnp.arange(owner_slots, dtype=jnp.int32) < owned_count
    arrived = lax.all_to_all(outgoing, "tensor", split_axis=2, concat_axis=2, tiled=True)
    arrived = arrived.reshape(owner_slots, 2, block_size, block_size)
    finished, new_rows, new_cols = precondition(
        arrived, eig_left, eig_right, row_stats, col_stats, in_use
    )
    returned = lax.all_to_all(
        finished.reshape(owner_slots, tensor_size, strip_rows * block_size),
        "tensor",
        split_axis=1,
        concat_axis=1,
        tiled=True,
    )
    update = jnp.einsum(
        "kpb,kpx->bx", selector, returned, preferred_element_type=jnp.float32
    ).astype(jnp.bfloat16)
    update = update.reshape(group_blocks, strip_rows, block_size)
    return (new_momentum, update, new_rows, new_cols)


def in_hbm(x):
    return pltpu.with_memory_space_constraint(x, pltpu.HBM)


def local(n_dp, n_tensor, gradient, momentum, eig_left, eig_right, row_stats, col_stats, owners):
    blocks, strip, size = gradient.shape
    slots = eig_left.shape[0]
    clip_norm = clip_share * size * math.sqrt(blocks * n_dp)
    anywhere = pl.BlockSpec(memory_space=pl.ANY)
    hbm = pl.BlockSpec(memory_space=pltpu.HBM)
    vmem = pl.BlockSpec(memory_space=pltpu.VMEM)
    square = (slots, size, size)
    pieces = (n_tensor, strip, size)
    ring = (columns, extra, strip, size)
    bands = (n_tensor // columns, chunk, size)
    shapes = (
        jax.ShapeDtypeStruct(momentum.shape, f32),
        jax.ShapeDtypeStruct(gradient.shape, bf16),
        jax.ShapeDtypeStruct(row_stats.shape, f32),
        jax.ShapeDtypeStruct(col_stats.shape, f32),
    )
    arguments = (owners.reshape(1, blocks), gradient, momentum)
    arguments += (eig_left, eig_right, row_stats, col_stats)
    *results, flags = pl.pallas_call(
        functools.partial(kernel, n_dp, n_tensor, clip_norm),
        out_shape=(*shapes, jax.ShapeDtypeStruct((1, 128), f32)),
        in_specs=[
            pl.BlockSpec(memory_space=pltpu.SMEM),
            hbm,
            hbm,
            hbm,
            hbm,
            vmem,
            vmem,
        ],
        out_specs=(anywhere, anywhere, vmem, vmem, vmem),
        scratch_shapes=[
            pltpu.VMEM(gradient.shape, bf16),
            pltpu.VMEM(gradient.shape, f32),
            pltpu.VMEM(gradient.shape, bf16),
            pltpu.VMEM(gradient.shape, bf16),
            pltpu.VMEM(square, bf16),
            pltpu.VMEM(square, bf16),
            pltpu.VMEM(square, bf16),
            pltpu.VMEM(square, bf16),
            pltpu.VMEM(square, f32),
            pltpu.VMEM(pieces, bf16),
            pltpu.VMEM(pieces, bf16),
            pltpu.VMEM(square, bf16),
            pltpu.VMEM(square, bf16),
            pltpu.VMEM(square, bf16),
            pltpu.VMEM((slots, *pieces), bf16),
            pltpu.VMEM(ring, bf16),
            pltpu.VMEM(ring, bf16),
            pltpu.VMEM(bands, bf16),
            pltpu.VMEM(bands, bf16),
            pltpu.VMEM((n_tensor, 1, 128), f32),
            pltpu.VMEM((n_dp, 1, 128), f32),
            pltpu.VMEM((1, 128), f32),
            pltpu.VMEM((8, 128), jnp.int32),
            pltpu.SMEM((8, 128), jnp.int32),
            pltpu.SemaphoreType.DMA((5,)),
            pltpu.SemaphoreType.DMA((9,)),
            pltpu.SemaphoreType.DMA((9,)),
            pltpu.SemaphoreType.DMA((2,)),
            pltpu.SemaphoreType.DMA((2, columns)),
        ],
        compiler_params=pltpu.CompilerParams(
            collective_id=0, has_side_effects=True, vmem_limit_bytes=48 << 20
        ),
        name="soap_step",
    )(*map(in_hbm, arguments))
    keep = pl.pallas_call(
        store,
        out_shape=shapes,
        in_specs=[anywhere] * 4,
        out_specs=(hbm,) * 4,
        scratch_shapes=[pltpu.SemaphoreType.DMA((4,))],
        compiler_params=pltpu.CompilerParams(vmem_limit_bytes=48 << 20),
        name="store",
    )
    inputs = (gradient, momentum, eig_left, eig_right, row_stats, col_stats, owners)
    results = lax.cond(
        flags[0, 127] > 0.5,
        lambda done, given: tuple(general(*given)),
        lambda done, given: done,
        tuple(results),
        inputs,
    )
    return keep(*results)


def solution(mesh):
    placed = (
        P("dp", "tensor", None),
        P("dp", "tensor", None),
        P(("dp", "tensor"), None, None),
        P(("dp", "tensor"), None, None),
        P(("dp", "tensor"), None),
        P(("dp", "tensor"), None),
        P("dp", None),
    )
    return jax.shard_map(
        functools.partial(local, mesh.shape["dp"], mesh.shape["tensor"]),
        mesh=mesh,
        in_specs=placed,
        out_specs=(
            P("dp", "tensor", None),
            P("dp", "tensor", None),
            P(("dp", "tensor"), None),
            P(("dp", "tensor"), None),
        ),
        check_vma=False,
    )
```
